256 devices in a mesh: blk: 64 (over x_lo, y, z), group: 4 (over x_hi, core).
Axes of the slice: x: 4 (x_hi: 2, x_lo: 2; x = x_hi * 2 + x_lo), y: 4, z: 8, core: 2. Of those that a mesh axis runs over, the one named last changes fastest.
Arguments:
- image: float32 [8192, 1152], P(('blk', 'group')), may hold values from -6 to 6
- text: float32 [8192, 1152], P(('blk', 'group')), may hold values from -6 to 6
- image_ids: int32 [8192], P(('blk', 'group')), may hold values from 0 to 1023
- text_ids: int32 [8192], P(('blk', 'group')), may hold values from 0 to 1023
- log_scale: float32 [1], replicated, may hold values from -4.1 to -3
- bias: float32 [1], replicated, may hold values from -2 to 0
Outputs:
- grad_image: float32 [8192, 1152], P(('blk', 'group'))
- grad_text: float32 [8192, 1152], P(('blk', 'group'))
- statistics: float32 [3], replicated
The draws below stay inside these ranges and needn't reach their ends.
All inputs are finite; a program needn't handle non-finite values.
Results may differ from the reference program's by a relative error of at most 0.0003.
Values sent between devices are 32-bit elements; how exact they have to be, the bound alone decides.
No kernel may reach another device: no remote copies, remote signals or barrier semaphores. Data moves between devices by JAX's collectives and lax.ppermute only.
A program may use at most 128 MiB of HBM per device.

```python
import jax
import jax.numpy as jnp
from jax import lax

D = 1152
TOTAL = 8192
CLASSES = 1024
N_BLK = 64


def with_ends(result, key, least, high):
    shape = result.shape
    spot = [jax.random.randint(jax.random.fold_in(key, axis), (), 0, shape[axis]) for axis in range(len(shape))]
    result = result.at[tuple(spot)].set(least)
    longest = shape.index(max(shape))
    spot[longest] = (spot[longest] + 1) % shape[longest]
    return result.at[tuple(spot)].set(high)


def block_scale(rng, extent, shards, smallest, top_value):
    loudness = 1.0
    for position, shards_of in shards:
        draws = jax.random.uniform(jax.random.fold_in(jax.random.fold_in(rng, 6), position), (shards_of,), jnp.float32, smallest / len(shards), top_value / len(shards))
        loudness = loudness * jnp.repeat(jnp.exp(draws), extent[position] // shards_of).reshape((-1,) + (1,) * (len(extent) - 1 - position))
    return loudness


def gaussian(own_key, dims, scale, reach, split=(), dtype=jnp.bfloat16):
    array = scale * jax.random.normal(own_key, dims, jnp.float32)
    if split:
        array = array * block_scale(own_key, dims, split, -0.22, 0.18)
    return jnp.clip(array, -reach, reach).astype(dtype)


def setup_inputs(seed: int = 0) -> dict:
    key_of = jax.random.split(jax.random.key(seed), 7)
    return {
        "image": gaussian(key_of[0], (TOTAL, D), 1.0, 6.0, ((0, 256),), jnp.float32),
        "text": gaussian(key_of[1], (TOTAL, D), 1.0, 6.0, ((0, 256),), jnp.float32),
        "image_ids": with_ends(jax.random.randint(key_of[2], (TOTAL,), 0, CLASSES), jax.random.fold_in(key_of[2], 1), 0, CLASSES - 1).astype(jnp.int32),
        "text_ids": with_ends(jax.random.randint(key_of[3], (TOTAL,), 0, CLASSES), jax.random.fold_in(key_of[3], 1), 0, CLASSES - 1).astype(jnp.int32),
        "log_scale": jnp.clip(jax.random.uniform(key_of[4], (1,), jnp.float32, -4.1, -3.0), -4.1, -3.0),
        "bias": jnp.clip(jax.random.uniform(key_of[5], (1,), jnp.float32, -2.0, 0.0), -2.0, 0.0),
    }


def reference(image, text, image_ids, text_ids, log_scale, bias):
    scale = jnp.exp(log_scale[0])
    offset = bias[0]
    total = image.shape[0]
    size = total // N_BLK
    blocks = image.reshape(N_BLK, size, image.shape[1])
    block_ids = image_ids.reshape(N_BLK, size)

    def step(carry, item):
        rows, tags = item
        dots = jnp.dot(rows, text.T, precision=lax.Precision.HIGHEST, preferred_element_type=jnp.float32)
        logits = scale * dots + offset
        labels = jnp.where(tags[:, None] == text_ids[None, :], 1.0, -1.0).astype(jnp.float32)
        margin = labels * logits
        losses = jax.nn.softplus(-margin)
        slope = -labels * jax.nn.sigmoid(-margin)
        weighted = scale * slope
        img_term = jnp.dot(weighted, text, precision=lax.Precision.HIGHEST, preferred_element_type=jnp.float32)
        txt_term = jnp.dot(weighted.T, rows, precision=lax.Precision.HIGHEST, preferred_element_type=jnp.float32)
        sums = jnp.stack([jnp.sum(losses), jnp.sum(slope * scale * dots), jnp.sum(slope)])
        return (carry[0] + txt_term, carry[1] + sums), img_term

    init = (jnp.zeros(text.shape, jnp.float32), jnp.zeros((3,), jnp.float32))
    (grad_text, sums), img_terms = lax.scan(step, init, (blocks, block_ids))
    grad_image = img_terms.reshape(image.shape)
    statistics = sums / (float(total) * float(total))
    return grad_image, grad_text, statistics
```

```python
import jax
import jax.numpy as jnp
from jax import lax
from jax.experimental import pallas as pl
from jax.experimental.pallas import tpu as pltpu
from jax.sharding import PartitionSpec as P

AXES = ("blk", "group")
NX, NY, NZ = 4, 4, 8
ROWS, D = 32, 1152
COLS = D // 128
MSG = ROWS // 8 * COLS + 1
HALF = ROWS // 16 * COLS
SIDE = 512
F32, BF16 = jnp.float32, jnp.bfloat16


def spot(x, y, z, c):
    return (((x % 2) * NY + y) * NZ + z) * 4 + (x // 2) * 2 + c


def table(move):
    pairs = []
    for x in range(NX):
        for y in range(NY):
            for z in range(NZ):
                for c in range(2):
                    a, b, d, e = move(x, y, z, c)
                    pairs.append((spot(x, y, z, c), spot(a % NX, b % NY, d % NZ, e)))
    return pairs


SWAP = table(lambda x, y, z, c: (x, y, z, 1 - c))


def along_z(way):
    return table(lambda x, y, z, c: (x, y, z + (way if c == 0 else -way), c))


def first(way):
    return table(lambda x, y, z, c: (x + way, y, z, c) if c == 0 else (x, y + way, z, c))


def second(way):
    return table(lambda x, y, z, c: (x, y + way, z, c) if c == 0 else (x + way, y, z, c))


FLIPS = (
    SWAP,
    table(lambda x, y, z, c: (x ^ 1, y, z, c)),
    table(lambda x, y, z, c: (3 - x, y, z, c)),
    table(lambda x, y, z, c: (x, y ^ 1, z, c)),
    table(lambda x, y, z, c: (x, 3 - y, z, c)),
    table(lambda x, y, z, c: (x, y, z ^ 1, c)),
    table(lambda x, y, z, c: (x, y, z ^ 2, c)),
    table(lambda x, y, z, c: (x, y, z ^ 4, c)),
)


def send(block, route):
    return lax.ppermute(block, AXES, route)


def pack(image_ref, text_ref, image_ids_ref, text_ids_ref, image_out, text_out):
    for rows, ids, out in ((image_ref, image_ids_ref, image_out), (text_ref, text_ids_ref, text_out)):
        for r in range(ROWS // 8):
            for c in range(COLS):
                at = r * COLS + c
                out[at + (1 if at >= HALF else 0)] = rows[8 * r : 8 * r + 8, 128 * c : 128 * c + 128]
        out[HALF] = jnp.zeros((8, 128), F32)
        out[HALF, 0:1, 0:ROWS] = ids[...].astype(F32)


def whole(operand, block):
    at = block * MSG
    return [(operand, at, at + HALF, 0, 16), (operand, at + HALF + 1, at + HALF, 16, 16)]


def halves(operand, at):
    return [(operand, at, at + HALF, 0, 16), (operand, at + HALF + 2, at + HALF + 1, 16, 16)]


IMAGE_SIZES = (64, 64, 64, 64, 32, 64, 64, 64, 32)
TEXT_SIZES = (128, 128, 128, 64, 64)
IMAGE_PARTS = [part for k, size in enumerate(IMAGE_SIZES) for b in range(size // 32) for part in whole(k, b)]
TEXT_PARTS = []
for k in range(3):
    TEXT_PARTS += whole(k, 0) + whole(k, 1) + whole(k, 2) + halves(k, 3 * MSG)
TEXT_PARTS += whole(3, 0) + whole(3, 1) + whole(4, 0) + halves(4, MSG)


def split(value):
    high = value.astype(BF16)
    return high, (value - high.astype(F32)).astype(BF16)


def fill(refs, parts, high, low, row):
    start = 0
    for operand, at, tag, lane, rows in parts:
        ref = refs[operand]
        for c in range(COLS):
            piece = jnp.concatenate([ref[at + c], ref[at + COLS + c]], axis=0)
            a, b = split(piece)
            high[start : start + 16, 128 * c : 128 * c + 128] = a
            low[start : start + 16, 128 * c : 128 * c + 128] = b
        row[0:1, start : start + rows] = ref[tag, 0:1, lane : lane + rows]
        start += rows


def dot3(a, b, dims):
    def one(p, q):
        return lax.dot_general(p, q, (dims, ((), ())), preferred_element_type=F32)

    return one(a[0], b[0]) + (one(a[0], b[1]) + one(a[1], b[0]))


N_IN = len(IMAGE_SIZES) + len(TEXT_SIZES)
CHUNK = 128


def visit(*refs):
    log_scale_ref, bias_ref = refs[0], refs[1]
    image_refs = refs[2 : 2 + len(IMAGE_SIZES)]
    text_refs = refs[2 + len(IMAGE_SIZES) : 2 + N_IN]
    outs = refs[2 + N_IN : 2 + 2 * N_IN]
    image_outs, text_outs = outs[: len(IMAGE_SIZES)], outs[len(IMAGE_SIZES) :]
    sums_ref = refs[2 + 2 * N_IN]
    ih, il, th, tl, irow, trow, wh, wl, gi = refs[3 + 2 * N_IN :]
    fill(image_refs, IMAGE_PARTS, ih, il, irow)
    fill(text_refs, TEXT_PARTS, th, tl, trow)
    scale = jnp.exp(log_scale_ref[...])
    offset = bias_ref[...]
    tags = jnp.transpose(jnp.broadcast_to(irow[0:1, :], (128, SIDE)))
    text_tags = trow[0:1, :]
    losses_sum = jnp.zeros((8, 128), F32)
    moment_sum = jnp.zeros((8, 128), F32)
    slope_sum = jnp.zeros((8, 128), F32)

    def fold(v):
        return jnp.sum(v.reshape(CHUNK // 8, 8, 128), axis=0)

    for k in range(SIDE // CHUNK):
        rows = slice(k * CHUNK, (k + 1) * CHUNK)
        dots = dot3((ih[rows, :], il[rows, :]), (th[...], tl[...]), ((1,), (1,)))
        for j in range(SIDE // 128):
            lanes = slice(128 * j, 128 * j + 128)
            moved = scale * dots[:, lanes]
            logits = moved + offset
            same = tags[rows, :] == text_tags[:, lanes]
            v = jnp.where(same, -logits, logits)
            e = jnp.exp(-jnp.abs(v))
            u = 1.0 + e
            r = 1.0 / u
            losses = jnp.maximum(v, 0.0) + (jnp.log(u) + (e - (u - 1.0)) * r)
            sig = jnp.where(v >= 0.0, r, e * r)
            slope = jnp.where(same, -sig, sig)
            losses_sum += fold(losses)
            moment_sum += fold(slope * moved)
            slope_sum += fold(slope)
            a, b = split(scale * slope)
            wh[rows, lanes] = a
            wl[rows, lanes] = b
        gi[rows, :] = dot3((wh[rows, :], wl[rows, :]), (th[...], tl[...]), ((1,), (0,)))
    start = 0
    for out, size in zip(image_outs, IMAGE_SIZES):
        out[...] = gi[start : start + size, :]
        start += size
    start = 0
    for out, size in zip(text_outs, TEXT_SIZES):
        cols = slice(start, start + size)
        out[...] = dot3((wh[:, cols], wl[:, cols]), (ih[...], il[...]), ((0,), (0,)))
        start += size
    sums_ref[...] = jnp.zeros((8, 128), F32)
    for k, total in enumerate((losses_sum, moment_sum, slope_sum)):
        sums_ref[k : k + 1, :] = jnp.broadcast_to(jnp.sum(total, keepdims=True), (1, 128))


def tiles(count):
    return jax.ShapeDtypeStruct((count, 8, 128), F32)


def rows_of(count):
    return jax.ShapeDtypeStruct((count, D), F32)


def vmem(count):
    return [pl.BlockSpec(memory_space=pltpu.VMEM)] * count


def shards(image, text, image_ids, text_ids, log_scale, bias):
    i0, t0 = pl.pallas_call(
        pack,
        out_shape=(tiles(MSG), tiles(MSG)),
        in_specs=vmem(4),
        out_specs=vmem(2),
    )(image, text, image_ids.reshape(1, ROWS), text_ids.reshape(1, ROWS))

    a = send(t0, first(1))
    b = send(t0, first(-1))
    o = send(i0, SWAP)
    c0 = jnp.concatenate([i0, o], axis=0)
    z1 = send(c0, along_z(1))
    a2 = send(a[: HALF + 1], first(1))
    b2 = send(b[HALF:], first(-1))
    z2 = send(z1, along_z(1))
    s1 = send(z1, SWAP)
    y0 = jnp.concatenate([t0, a, b, a2, b2], axis=0)
    yp = send(y0, second(1))
    ym = send(y0, second(-1))
    z3 = send(z2, along_z(1))
    s2 = send(z2, SWAP)
    y2a = send(yp[: 2 * MSG], second(1))
    y2b = send(ym[2 * MSG :], second(-1))
    z4 = send(z3[:MSG], along_z(1))
    s3 = send(z3, SWAP)
    s4 = send(z4, SWAP)

    sizes = IMAGE_SIZES + TEXT_SIZES
    outs = pl.pallas_call(
        visit,
        out_shape=tuple(rows_of(n) for n in sizes) + (jax.ShapeDtypeStruct((8, 128), F32),),
        in_specs=vmem(2 + N_IN),
        out_specs=tuple(vmem(N_IN + 1)),
        scratch_shapes=[pltpu.VMEM((SIDE, D), BF16)] * 4
        + [pltpu.VMEM((8, SIDE), F32)] * 2
        + [pltpu.VMEM((SIDE, SIDE), BF16)] * 2
        + [pltpu.VMEM((SIDE, D), F32)],
        compiler_params=pltpu.CompilerParams(vmem_limit_bytes=44 * 2**20),
        cost_estimate=pl.CostEstimate(
            flops=9 * 2 * SIDE * SIDE * D, bytes_accessed=4 * 4 * SIDE * D, transcendentals=3 * SIDE * SIDE
        ),
    )(log_scale.reshape(1, 1), bias.reshape(1, 1), c0, z1, z2, z3, z4, s1, s2, s3, s4, y0, yp, ym, y2a, y2b)
    gc, g1, g2, g3, g4, h1, h2, h3, h4, k0, kp, km, k2a, k2b, sums = outs

    r2a = send(k2a, second(-1))
    r2b = send(k2b, second(1))
    g4 = g4 + send(h4, SWAP)
    q3 = send(h3, SWAP)
    q2 = send(h2, SWAP)
    q1 = send(h1, SWAP)
    w4 = send(g4, along_z(-1))
    kp = jnp.concatenate([kp[:64] + r2a, kp[64:]], axis=0)
    km = jnp.concatenate([km[:64], km[64:] + r2b], axis=0)
    rp = send(kp, second(-1))
    rm = send(km, second(1))
    g3 = g3 + q3 + jnp.pad(w4, ((0, 32), (0, 0)))
    w3 = send(g3, along_z(-1))
    g2 = g2 + q2 + w3
    w2 = send(g2, along_z(-1))
    g1 = g1 + q1 + w2
    k0 = k0 + rp + rm
    x2a = send(k0[96:112], first(-1))
    x2b = send(k0[112:128], first(1))
    w1 = send(g1, along_z(-1))
    ka = k0[32:64] + jnp.pad(x2a, ((0, 16), (0, 0)))
    kb = k0[64:96] + jnp.pad(x2b, ((16, 0), (0, 0)))
    ra = send(ka, first(-1))
    rb = send(kb, first(1))
    gc = gc + w1
    other = send(gc[32:], SWAP)
    grad_image = gc[:32] + other
    grad_text = k0[:32] + ra + rb

    for route in FLIPS:
        sums = sums + send(sums, route)
    statistics = sums[:3, 0] * (2.0**-26)
    return grad_image, grad_text, statistics


def solution(mesh):
    rows, ids = P(AXES, None), P(AXES)
    return jax.shard_map(
        shards,
        mesh=mesh,
        in_specs=(rows, rows, ids, ids, P(), P()),
        out_specs=(rows, rows, P()),
        check_vma=False,
    )
```

```python
import jax
import jax.numpy as jnp
from jax import lax
from jax.experimental import pallas as pl
from jax.experimental.pallas import tpu as pltpu
from jax.sharding import PartitionSpec as P

AXES = ("blk", "group")
NX, NY, NZ = 4, 4, 8
ROWS, D = 32, 1152
COLS = D // 128
MSG = ROWS // 8 * COLS + 1
HALF = ROWS // 16 * COLS
SIDE = 512
F32, BF16 = jnp.float32, jnp.bfloat16


def spot(x, y, z, c):
    return (((x % 2) * NY + y) * NZ + z) * 4 + (x // 2) * 2 + c


def table(move):
    pairs = []
    for x in range(NX):
        for y in range(NY):
            for z in range(NZ):
                for c in range(2):
                    a, b, d, e = move(x, y, z, c)
                    pairs.append((spot(x, y, z, c), spot(a % NX, b % NY, d % NZ, e)))
    return pairs


SWAP = table(lambda x, y, z, c: (x, y, z, 1 - c))


def along_z(way):
    return table(lambda x, y, z, c: (x, y, z + (way if c == 0 else -way), c))


def first(way):
    return table(lambda x, y, z, c: (x + way, y, z, c) if c == 0 else (x, y + way, z, c))


def second(way):
    return table(lambda x, y, z, c: (x, y + way, z, c) if c == 0 else (x + way, y, z, c))


def send(block, route):
    return lax.ppermute(block, AXES, route)


def pack(image_ref, text_ref, image_ids_ref, text_ids_ref, image_out, text_out):
    for rows, ids, out in ((image_ref, image_ids_ref, image_out), (text_ref, text_ids_ref, text_out)):
        for r in range(ROWS // 8):
            for c in range(COLS):
                at = r * COLS + c
                out[at + (1 if at >= HALF else 0)] = rows[8 * r : 8 * r + 8, 128 * c : 128 * c + 128]
        out[HALF] = jnp.zeros((8, 128), F32)
        out[HALF, 0:1, 0:ROWS] = ids[...].astype(F32)


def whole(operand, block):
    at = block * MSG
    return [(operand, at, at + HALF, 0, 16), (operand, at + HALF + 1, at + HALF, 16, 16)]


IMAGE_SIZES = (64, 64, 64, 64, 32, 64, 64, 64, 32)
TEXT_SIZES = (128, 128, 128, 64, 64)
IMAGE_PARTS = [part for k, size in enumerate(IMAGE_SIZES) for b in range(size // 32) for part in whole(k, b)]
TEXT_PARTS = [part for k, size in enumerate(TEXT_SIZES) for b in range(size // 32) for part in whole(k, b)]
IMAGE_STARTS = tuple(sum(IMAGE_SIZES[:k]) for k in range(len(IMAGE_SIZES)))
TEXT_STARTS = tuple(sum(TEXT_SIZES[:k]) for k in range(len(TEXT_SIZES)))
N_IMAGE, N_TEXT = len(IMAGE_SIZES), len(TEXT_SIZES)


def split(value):
    high = value.astype(BF16)
    return high, (value - high.astype(F32)).astype(BF16)


def fill(refs, parts, high, low, row):
    start = 0
    for operand, at, tag, lane, rows in parts:
        ref = refs[operand]
        for c in range(COLS):
            piece = jnp.concatenate([ref[at + c], ref[at + COLS + c]], axis=0)
            a, b = split(piece)
            high[start : start + 16, 128 * c : 128 * c + 128] = a
            low[start : start + 16, 128 * c : 128 * c + 128] = b
        row[0:1, start : start + rows] = ref[tag, 0:1, lane : lane + rows]
        start += rows


def dot3(a, b, dims):
    def one(p, q):
        return lax.dot_general(p, q, (dims, ((), ())), preferred_element_type=F32)

    return one(a[0], b[0]) + (one(a[0], b[1]) + one(a[1], b[0]))


CHUNK = 128


def emit(out, rows, sums):
    for r in range(rows.shape[0] // 8):
        for c in range(COLS):
            at = r * COLS + c
            out[at + (1 if r >= ROWS // 8 else 0)] = rows[8 * r : 8 * r + 8, 128 * c : 128 * c + 128]
    out[MSG - 1] = sums


def gradients(image_pieces, text_pieces, held, sums, outs):
    ih, il, th, tl, wh, wl = held
    for out, k in zip(outs, image_pieces):
        rows = slice(IMAGE_STARTS[k], IMAGE_STARTS[k] + IMAGE_SIZES[k])
        share = 0.5 if IMAGE_SIZES[k] == 32 else 1.0
        emit(out, dot3((wh[rows, :], wl[rows, :]), (th[...], tl[...]), ((1,), (0,))), share * sums)
    for out, k in zip(outs[len(image_pieces) :], text_pieces):
        cols = slice(TEXT_STARTS[k], TEXT_STARTS[k] + TEXT_SIZES[k])
        out[...] = dot3((wh[:, cols], wl[:, cols]), (ih[...], il[...]), ((0,), (0,)))


def visit(image_pieces, text_pieces, *refs):
    log_scale_ref, bias_ref, place_ref = refs[:3]
    refs = refs[3:]
    image_refs = refs[:N_IMAGE]
    text_refs = refs[N_IMAGE : N_IMAGE + N_TEXT]
    ih, il, th, tl, wh, wl, sums_ref, *outs, irow, trow = refs[N_IMAGE + N_TEXT :]
    fill(image_refs, IMAGE_PARTS, ih, il, irow)
    fill(text_refs, TEXT_PARTS, th, tl, trow)
    scale = jnp.exp(log_scale_ref[...])
    offset = bias_ref[...]
    tags = jnp.transpose(jnp.broadcast_to(irow[0:1, :], (128, SIDE)))
    text_tags = trow[0:1, :]
    losses_sum = jnp.zeros((8, 128), F32)
    moment_sum = jnp.zeros((8, 128), F32)
    slope_sum = jnp.zeros((8, 128), F32)

    def fold(v):
        return jnp.sum(v.reshape(CHUNK // 8, 8, 128), axis=0)

    for k in range(SIDE // CHUNK):
        rows = slice(k * CHUNK, (k + 1) * CHUNK)
        dots = dot3((ih[rows, :], il[rows, :]), (th[...], tl[...]), ((1,), (1,)))
        for j in range(SIDE // 128):
            lanes = slice(128 * j, 128 * j + 128)
            moved = scale * dots[:, lanes]
            logits = moved + offset
            same = tags[rows, :] == text_tags[:, lanes]
            v = jnp.where(same, -logits, logits)
            e = jnp.exp(-jnp.abs(v))
            u = 1.0 + e
            r = 1.0 / u
            losses = jnp.maximum(v, 0.0) + (jnp.log(u) + (e - (u - 1.0)) * r)
            sig = jnp.where(v >= 0.0, r, e * r)
            slope = jnp.where(same, -sig, sig)
            losses_sum += fold(losses)
            moment_sum += fold(slope * moved)
            slope_sum += fold(slope)
            a, b = split(scale * slope)
            wh[rows, lanes] = a
            wl[rows, lanes] = b
    row = lax.broadcasted_iota(jnp.int32, (8, 128), 0)
    lane = lax.broadcasted_iota(jnp.int32, (8, 128), 1)
    mine = lane + 128 * (row % 2) == place_ref[...]
    sums = jnp.zeros((8, 128), F32)
    for k, total in enumerate((losses_sum, moment_sum, slope_sum)):
        sums = jnp.where(mine & (row // 2 == k), jnp.sum(total, keepdims=True), sums)
    sums_ref[...] = sums
    gradients(image_pieces, text_pieces, (ih, il, th, tl, wh, wl), sums, outs)


def later(image_pieces, text_pieces, *refs):
    gradients(image_pieces, text_pieces, refs[:6], refs[6][...], refs[7:])


def unpack(kept_ref, came_ref, other_ref, rows_out, sums_out):
    for r in range(ROWS // 8):
        for c in range(COLS):
            at = r * COLS + c
            rows_out[8 * r : 8 * r + 8, 128 * c : 128 * c + 128] = kept_ref[at] + came_ref[at] + other_ref[1 + at]
    sums_out[...] = kept_ref[MSG - 1] + came_ref[MSG - 1] + other_ref[0]


def tiles(count):
    return jax.ShapeDtypeStruct((count, 8, 128), F32)


def rows_of(count):
    return jax.ShapeDtypeStruct((count, D), F32)


def vmem(count):
    return [pl.BlockSpec(memory_space=pltpu.VMEM)] * count


def cost(products, operands):
    return pl.CostEstimate(flops=6 * products, bytes_accessed=operands, transcendentals=0)


def shapes_of(image_pieces, text_pieces):
    return tuple(tiles(IMAGE_SIZES[k] // 8 * COLS + 1) for k in image_pieces) + tuple(
        rows_of(TEXT_SIZES[k]) for k in text_pieces
    )


def returned(held, image_pieces, text_pieces):
    shapes = shapes_of(image_pieces, text_pieces)
    count = sum(IMAGE_SIZES[k] for k in image_pieces) + sum(TEXT_SIZES[k] for k in text_pieces)
    return pl.pallas_call(
        lambda *refs: later(image_pieces, text_pieces, *refs),
        out_shape=shapes,
        in_specs=vmem(7),
        out_specs=tuple(vmem(len(shapes))),
        compiler_params=pltpu.CompilerParams(vmem_limit_bytes=40 * 2**20),
        cost_estimate=cost(count * SIDE * D, 4 * SIDE * D),
    )(*held)


def put(block, top, bottom):
    return jnp.pad(block, ((top, bottom),) + ((0, 0),) * (block.ndim - 1))


def shards(image, text, image_ids, text_ids, log_scale, bias):
    i0, t0 = pl.pallas_call(
        pack,
        out_shape=(tiles(MSG), tiles(MSG)),
        in_specs=vmem(4),
        out_specs=tuple(vmem(2)),
    )(image, text, image_ids.reshape(1, ROWS), text_ids.reshape(1, ROWS))

    c0 = jnp.concatenate([i0, send(i0, SWAP)], axis=0)
    z1 = send(c0, along_z(1))
    a = send(t0, first(1))
    b = send(t0, first(-1))
    c = send(t0, first(2))
    y0 = jnp.concatenate([t0, a, b, c], axis=0)
    z2 = send(z1, along_z(1))
    s1 = send(z1, SWAP)
    yp = send(y0, second(1))
    ym = send(y0, second(-1))
    z3 = send(z2, along_z(1))
    s2 = send(z2, SWAP)
    y2a = send(yp[: 2 * MSG], second(1))
    y2b = send(ym[2 * MSG :], second(-1))
    z4 = send(z3[:MSG], along_z(1))
    s3 = send(z3, SWAP)
    s4 = send(z4, SWAP)

    wide = jax.ShapeDtypeStruct((SIDE, D), BF16)
    square = jax.ShapeDtypeStruct((SIDE, SIDE), BF16)
    early = shapes_of((4, 8), (3, 4))
    place = lax.axis_index("blk") * 4 + lax.axis_index("group")
    *held, g4, h4, k2a, k2b = pl.pallas_call(
        lambda *refs: visit((4, 8), (3, 4), *refs),
        out_shape=(wide,) * 4 + (square,) * 2 + (jax.ShapeDtypeStruct((8, 128), F32),) + early,
        in_specs=vmem(3 + N_IMAGE + N_TEXT),
        out_specs=tuple(vmem(7 + len(early))),
        scratch_shapes=[pltpu.VMEM((8, SIDE), F32)] * 2,
        compiler_params=pltpu.CompilerParams(vmem_limit_bytes=40 * 2**20),
        cost_estimate=cost(SIDE * (SIDE + 192) * D, 8 * SIDE * D),
    )(
        log_scale.reshape(1, 1), bias.reshape(1, 1), place.reshape(1, 1),
        c0, z1, z2, z3, z4, s1, s2, s3, s4,
        y0, yp, ym, y2a, y2b,
    )

    q4 = send(h4, SWAP)
    r2a = send(k2a, second(-1))
    r2b = send(k2b, second(1))
    w4 = send(g4 + q4, along_z(-1))
    g3, h3, kp, km = returned(held, (3, 7), (1, 2))
    q3 = send(h3, SWAP)
    w3 = send(g3 + q3 + put(w4, 0, MSG - 1), along_z(-1))
    rp = send(kp + put(r2a, 0, 64), second(-1))
    rm = send(km + put(r2b, 64, 0), second(1))
    g2, h2, g1, h1, gc, k0 = returned(held, (2, 6, 1, 5, 0), (0,))
    q2 = send(h2, SWAP)
    q1 = send(h1, SWAP)
    w2 = send(g2 + q2 + w3, along_z(-1))
    w1 = send(g1 + q1 + w2, along_z(-1))
    k0 = k0 + rp + rm
    ra = send(k0[32:64], first(-1))
    rb = send(k0[64:96], first(1))
    rc = send(k0[96:128], first(2))
    grad_text = k0[:32] + ra + rb + rc
    other = send(gc[MSG - 1 :] + w1[MSG - 1 :], SWAP)
    grad_image, sums = pl.pallas_call(
        unpack,
        out_shape=(rows_of(ROWS), jax.ShapeDtypeStruct((8, 128), F32)),
        in_specs=vmem(3),
        out_specs=tuple(vmem(2)),
    )(gc, w1, other)
    for route in (first, second):
        sums = (sums + send(sums, route(2))) + (send(sums, route(1)) + send(sums, route(-1)))
    statistics = jnp.sum(sums[:6].reshape(3, 256), axis=1) * (2.0**-26)
    return grad_image, grad_text, statistics


def solution(mesh):
    rows, ids = P(AXES, None), P(AXES)
    return jax.shard_map(
        shards,
        mesh=mesh,
        in_specs=(rows, rows, ids, ids, P(), P()),
        out_specs=(rows, rows, P()),
        check_vma=False,
    )
```

```python
import jax
import jax.numpy as jnp
from jax import lax
from jax.experimental import pallas as pl
from jax.experimental.pallas import tpu as pltpu
from jax.sharding import PartitionSpec as P

AXES = ("blk", "group")
NX, NY, NZ = 4, 4, 8
ROWS, D = 32, 1152
COLS = D // 128
MSG = ROWS // 8 * COLS + 1
HALF = ROWS // 16 * COLS
SIDE = 512
F32, BF16 = jnp.float32, jnp.bfloat16


def spot(x, y, z, c):
    return (((x % 2) * NY + y) * NZ + z) * 4 + (x // 2) * 2 + c


def table(move):
    pairs = []
    for x in range(NX):
        for y in range(NY):
            for z in range(NZ):
                for c in range(2):
                    a, b, d, e = move(x, y, z, c)
                    pairs.append((spot(x, y, z, c), spot(a % NX, b % NY, d % NZ, e)))
    return pairs


SWAP = table(lambda x, y, z, c: (x, y, z, 1 - c))


def along_z(way):
    return table(lambda x, y, z, c: (x, y, z + (way if c == 0 else -way), c))


def first(way):
    return table(lambda x, y, z, c: (x + way, y, z, c) if c == 0 else (x, y + way, z, c))


def second(way):
    return table(lambda x, y, z, c: (x, y + way, z, c) if c == 0 else (x + way, y, z, c))


def send(block, route):
    return lax.ppermute(block, AXES, route)


def pack(image_ref, text_ref, image_ids_ref, text_ids_ref, image_out, text_out):
    for rows, ids, out in ((image_ref, image_ids_ref, image_out), (text_ref, text_ids_ref, text_out)):
        for r in range(ROWS // 8):
            for c in range(COLS):
                at = r * COLS + c
                out[at + (1 if at >= HALF else 0)] = rows[8 * r : 8 * r + 8, 128 * c : 128 * c + 128]
        out[HALF] = jnp.zeros((8, 128), F32)
        out[HALF, 0:1, 0:ROWS] = ids[...].astype(F32)


def whole(operand, block):
    at = block * MSG
    return [(operand, at, at + HALF, 0, 16), (operand, at + HALF + 1, at + HALF, 16, 16)]


IMAGE_SIZES = (64, 64, 64, 64, 32, 64, 64, 64, 32)
TEXT_SIZES = (128, 128, 128, 64, 64)
IMAGE_PARTS = [part for k, size in enumerate(IMAGE_SIZES) for b in range(size // 32) for part in whole(k, b)]
TEXT_PARTS = [part for k, size in enumerate(TEXT_SIZES) for b in range(size // 32) for part in whole(k, b)]
IMAGE_STARTS = tuple(sum(IMAGE_SIZES[:k]) for k in range(len(IMAGE_SIZES)))
TEXT_STARTS = tuple(sum(TEXT_SIZES[:k]) for k in range(len(TEXT_SIZES)))
PIECES = range(len(IMAGE_SIZES))
N_IMAGE, N_TEXT = len(IMAGE_SIZES), len(TEXT_SIZES)


def split(value):
    high = value.astype(BF16)
    return high, (value - high.astype(F32)).astype(BF16)


def fill(refs, parts, high, low, row):
    start = 0
    for operand, at, tag, lane, rows in parts:
        ref = refs[operand]
        for c in range(COLS):
            piece = jnp.concatenate([ref[at + c], ref[at + COLS + c]], axis=0)
            a, b = split(piece)
            high[start : start + 16, 128 * c : 128 * c + 128] = a
            low[start : start + 16, 128 * c : 128 * c + 128] = b
        row[0:1, start : start + rows] = ref[tag, 0:1, lane : lane + rows]
        start += rows


def dot3(a, b, dims):
    def one(p, q):
        return lax.dot_general(p, q, (dims, ((), ())), preferred_element_type=F32)

    return one(a[0], b[0]) + (one(a[0], b[1]) + one(a[1], b[0]))


CHUNK = 128


def emit(out, rows, sums):
    for r in range(rows.shape[0] // 8):
        for c in range(COLS):
            at = r * COLS + c
            out[at + (1 if r >= ROWS // 8 else 0)] = rows[8 * r : 8 * r + 8, 128 * c : 128 * c + 128]
    out[MSG - 1] = sums


def gradients(image_pieces, text_pieces, held, sums, outs):
    ih, il, th, tl, wh, wl = held
    for group in ((0, 1, 2, 3), (4, 5, 6, 7, 8)):
        at = IMAGE_STARTS[group[0]]
        rows = slice(at, at + sum(IMAGE_SIZES[k] for k in group))
        terms = dot3((wh[rows, :], wl[rows, :]), (th[...], tl[...]), ((1,), (0,)))
        for k in group:
            first_row = IMAGE_STARTS[k] - at
            share = 0.5 if IMAGE_SIZES[k] == 32 else 1.0
            emit(outs[k], terms[first_row : first_row + IMAGE_SIZES[k], :], share * sums)
    for out, k in zip(outs[len(image_pieces) :], text_pieces):
        cols = slice(TEXT_STARTS[k], TEXT_STARTS[k] + TEXT_SIZES[k])
        out[...] = dot3((wh[:, cols], wl[:, cols]), (ih[...], il[...]), ((0,), (0,)))


def visit(image_pieces, text_pieces, *refs):
    log_scale_ref, bias_ref, place_ref = refs[:3]
    refs = refs[3:]
    image_refs = refs[:N_IMAGE]
    text_refs = refs[N_IMAGE : N_IMAGE + N_TEXT]
    sums_ref, *outs, ih, il, th, tl, wh, wl, irow, trow = refs[N_IMAGE + N_TEXT :]
    fill(image_refs, IMAGE_PARTS, ih, il, irow)
    fill(text_refs, TEXT_PARTS, th, tl, trow)
    scale = jnp.exp(log_scale_ref[...])
    offset = bias_ref[...]
    tags = jnp.transpose(jnp.broadcast_to(irow[0:1, :], (128, SIDE)))
    text_tags = trow[0:1, :]
    losses_sum = jnp.zeros((8, 128), F32)
    moment_sum = jnp.zeros((8, 128), F32)
    slope_sum = jnp.zeros((8, 128), F32)

    def fold(v):
        return jnp.sum(v.reshape(CHUNK // 8, 8, 128), axis=0)

    for k in range(SIDE // CHUNK):
        rows = slice(k * CHUNK, (k + 1) * CHUNK)
        dots = dot3((ih[rows, :], il[rows, :]), (th[...], tl[...]), ((1,), (1,)))
        for j in range(SIDE // 128):
            lanes = slice(128 * j, 128 * j + 128)
            moved = scale * dots[:, lanes]
            logits = moved + offset
            same = tags[rows, :] == text_tags[:, lanes]
            v = jnp.where(same, -logits, logits)
            e = jnp.exp(-jnp.abs(v))
            u = 1.0 + e
            r = 1.0 / u
            losses = jnp.maximum(v, 0.0) + (jnp.log(u) + (e - (u - 1.0)) * r)
            sig = jnp.where(v >= 0.0, r, e * r)
            slope = jnp.where(same, -sig, sig)
            losses_sum += fold(losses)
            moment_sum += fold(slope * moved)
            slope_sum += fold(slope)
            a, b = split(scale * slope)
            wh[rows, lanes] = a
            wl[rows, lanes] = b
    row = lax.broadcasted_iota(jnp.int32, (8, 128), 0)
    lane = lax.broadcasted_iota(jnp.int32, (8, 128), 1)
    mine = lane + 128 * (row % 2) == place_ref[...]
    sums = jnp.zeros((8, 128), F32)
    for k, total in enumerate((losses_sum, moment_sum, slope_sum)):
        sums = jnp.where(mine & (row // 2 == k), jnp.sum(total, keepdims=True), sums)
    sums_ref[...] = sums
    gradients(image_pieces, text_pieces, (ih, il, th, tl, wh, wl), sums, outs)


def unpack(kept_ref, came_ref, other_ref, rows_out, sums_out):
    for r in range(ROWS // 8):
        for c in range(COLS):
            at = r * COLS + c
            rows_out[8 * r : 8 * r + 8, 128 * c : 128 * c + 128] = kept_ref[at] + came_ref[at] + other_ref[1 + at]
    sums_out[...] = kept_ref[MSG - 1] + came_ref[MSG - 1] + other_ref[0]


def tiles(count):
    return jax.ShapeDtypeStruct((count, 8, 128), F32)


def rows_of(count):
    return jax.ShapeDtypeStruct((count, D), F32)


def vmem(count):
    return [pl.BlockSpec(memory_space=pltpu.VMEM)] * count


def cost(products, operands):
    return pl.CostEstimate(flops=6 * products, bytes_accessed=operands, transcendentals=0)


def shapes_of(image_pieces, text_pieces):
    return tuple(tiles(IMAGE_SIZES[k] // 8 * COLS + 1) for k in image_pieces) + tuple(
        rows_of(TEXT_SIZES[k]) for k in text_pieces
    )


def put(block, top, bottom):
    return jnp.pad(block, ((top, bottom),) + ((0, 0),) * (block.ndim - 1))


def shards(image, text, image_ids, text_ids, log_scale, bias):
    i0, t0 = pl.pallas_call(
        pack,
        out_shape=(tiles(MSG), tiles(MSG)),
        in_specs=vmem(4),
        out_specs=tuple(vmem(2)),
    )(image, text, image_ids.reshape(1, ROWS), text_ids.reshape(1, ROWS))

    c0 = jnp.concatenate([i0, send(i0, SWAP)], axis=0)
    z1 = send(c0, along_z(1))
    a = send(t0, first(1))
    b = send(t0, first(-1))
    c = send(t0, first(2))
    y0 = jnp.concatenate([t0, a, b, c], axis=0)
    z2 = send(z1, along_z(1))
    s1 = send(z1, SWAP)
    yp = send(y0, second(1))
    ym = send(y0, second(-1))
    z3 = send(z2, along_z(1))
    s2 = send(z2, SWAP)
    y2a = send(yp[: 2 * MSG], second(1))
    y2b = send(ym[2 * MSG :], second(-1))
    z4 = send(z3[:MSG], along_z(1))
    s3 = send(z3, SWAP)
    s4 = send(z4, SWAP)

    early = shapes_of(PIECES, range(N_TEXT))
    place = lax.axis_index("blk") * 4 + lax.axis_index("group")
    *_, gc, g1, g2, g3, g4, h1, h2, h3, h4, k0, kp, km, k2a, k2b = pl.pallas_call(
        lambda *refs: visit(PIECES, range(N_TEXT), *refs),
        out_shape=(jax.ShapeDtypeStruct((8, 128), F32),) + early,
        in_specs=vmem(3 + N_IMAGE + N_TEXT),
        out_specs=tuple(vmem(1 + len(early))),
        scratch_shapes=[pltpu.VMEM((SIDE, D), BF16)] * 4
        + [pltpu.VMEM((SIDE, SIDE), BF16)] * 2
        + [pltpu.VMEM((8, SIDE), F32)] * 2,
        compiler_params=pltpu.CompilerParams(vmem_limit_bytes=40 * 2**20),
        cost_estimate=cost(3 * SIDE * SIDE * D, 8 * SIDE * D),
    )(
        log_scale.reshape(1, 1), bias.reshape(1, 1), place.reshape(1, 1),
        c0, z1, z2, z3, z4, s1, s2, s3, s4,
        y0, yp, ym, y2a, y2b,
    )

    q4 = send(h4, SWAP)
    r2a = send(k2a, second(-1))
    r2b = send(k2b, second(1))
    w4 = send(g4 + q4, along_z(-1))
    q3 = send(h3, SWAP)
    w3 = send(g3 + q3 + put(w4, 0, MSG - 1), along_z(-1))
    rp = send(kp + put(r2a, 0, 64), second(-1))
    rm = send(km + put(r2b, 64, 0), second(1))
    q2 = send(h2, SWAP)
    q1 = send(h1, SWAP)
    w2 = send(g2 + q2 + w3, along_z(-1))
    w1 = send(g1 + q1 + w2, along_z(-1))
    k0 = k0 + rp + rm
    ra = send(k0[32:64], first(-1))
    rb = send(k0[64:96], first(1))
    rc = send(k0[96:128], first(2))
    grad_text = k0[:32] + ra + rb + rc
    other = send(gc[MSG - 1 :] + w1[MSG - 1 :], SWAP)
    grad_image, sums = pl.pallas_call(
        unpack,
        out_shape=(rows_of(ROWS), jax.ShapeDtypeStruct((8, 128), F32)),
        in_specs=vmem(3),
        out_specs=tuple(vmem(2)),
        compiler_params=pltpu.CompilerParams(vmem_limit_bytes=2 * 2**20),
    )(gc, w1, other)
    for route in (first, second):
        sums = (sums + send(sums, route(2))) + (send(sums, route(1)) + send(sums, route(-1)))
    statistics = jnp.sum(sums[:6].reshape(3, 256), axis=1) * (2.0**-26)
    return grad_image, grad_text, statistics


def solution(mesh):
    rows, ids = P(AXES, None), P(AXES)
    return jax.shard_map(
        shards,
        mesh=mesh,
        in_specs=(rows, rows, ids, ids, P(), P()),
        out_specs=(rows, rows, P()),
        check_vma=False,
    )
```

```python
import jax
import jax.numpy as jnp
from jax import lax
from jax.experimental import pallas as pl
from jax.experimental.pallas import tpu as pltpu
from jax.sharding import PartitionSpec as P

AXES = ("blk", "group")
NX, NY, NZ = 4, 4, 8
ROWS, D = 32, 1152
COLS = D // 128
MSG = ROWS // 8 * COLS + 1
HALF = ROWS // 16 * COLS
SIDE = 512
F32, BF16 = jnp.float32, jnp.bfloat16


def spot(x, y, z, c):
    return (((x % 2) * NY + y) * NZ + z) * 4 + (x // 2) * 2 + c


def table(move):
    pairs = []
    for x in range(NX):
        for y in range(NY):
            for z in range(NZ):
                for c in range(2):
                    a, b, d, e = move(x, y, z, c)
                    pairs.append((spot(x, y, z, c), spot(a % NX, b % NY, d % NZ, e)))
    return pairs


SWAP = table(lambda x, y, z, c: (x, y, z, 1 - c))


def along_z(way):
    return table(lambda x, y, z, c: (x, y, z + (way if c == 0 else -way), c))


def first(way):
    return table(lambda x, y, z, c: (x + way, y, z, c) if c == 0 else (x, y + way, z, c))


def second(way):
    return table(lambda x, y, z, c: (x, y + way, z, c) if c == 0 else (x + way, y, z, c))


def send(block, route):
    return lax.ppermute(block, AXES, route)


def pack(image_ref, text_ref, image_ids_ref, text_ids_ref, image_out, text_out):
    for rows, ids, out in ((image_ref, image_ids_ref, image_out), (text_ref, text_ids_ref, text_out)):
        for r in range(ROWS // 8):
            for c in range(COLS):
                at = r * COLS + c
                out[at + (1 if at >= HALF else 0)] = rows[8 * r : 8 * r + 8, 128 * c : 128 * c + 128]
        out[HALF] = jnp.zeros((8, 128), F32)
        out[HALF, 0:1, 0:ROWS] = ids[...].astype(F32)


def whole(operand, block):
    at = block * MSG
    return [(operand, at, at + HALF, 0, 16), (operand, at + HALF + 1, at + HALF, 16, 16)]


IMAGE_SIZES = (64, 64, 64, 64, 32, 64, 64, 64, 32)
TEXT_SIZES = (128, 128, 128, 64, 64)
IMAGE_PARTS = [part for k, size in enumerate(IMAGE_SIZES) for b in range(size // 32) for part in whole(k, b)]
TEXT_PARTS = [part for k, size in enumerate(TEXT_SIZES) for b in range(size // 32) for part in whole(k, b)]
IMAGE_STARTS = tuple(sum(IMAGE_SIZES[:k]) for k in range(len(IMAGE_SIZES)))
TEXT_STARTS = tuple(sum(TEXT_SIZES[:k]) for k in range(len(TEXT_SIZES)))
PIECES = range(len(IMAGE_SIZES))
N_IMAGE, N_TEXT = len(IMAGE_SIZES), len(TEXT_SIZES)


def split(value):
    high = value.astype(BF16)
    return high, (value - high.astype(F32)).astype(BF16)


def fill(refs, parts, high, low, row):
    start = 0
    for operand, at, tag, lane, rows in parts:
        ref = refs[operand]
        for c in range(COLS):
            piece = jnp.concatenate([ref[at + c], ref[at + COLS + c]], axis=0)
            a, b = split(piece)
            high[start : start + 16, 128 * c : 128 * c + 128] = a
            low[start : start + 16, 128 * c : 128 * c + 128] = b
        row[0:1, start : start + rows] = ref[tag, 0:1, lane : lane + rows]
        start += rows


def dot3(a, b, dims):
    def one(p, q):
        return lax.dot_general(p, q, (dims, ((), ())), preferred_element_type=F32)

    return one(a[0], b[0]) + (one(a[0], b[1]) + one(a[1], b[0]))


CHUNK = 256


def emit(out, rows, sums):
    for r in range(rows.shape[0] // 8):
        for c in range(COLS):
            at = r * COLS + c
            out[at + (1 if r >= ROWS // 8 else 0)] = rows[8 * r : 8 * r + 8, 128 * c : 128 * c + 128]
    out[MSG - 1] = sums


def gradients(image_pieces, text_pieces, held, sums, outs):
    ih, il, th, tl, wh, wl = held
    for group in ((0, 1, 2, 3), (4, 5, 6, 7, 8)):
        at = IMAGE_STARTS[group[0]]
        rows = slice(at, at + sum(IMAGE_SIZES[k] for k in group))
        terms = dot3((wh[rows, :], wl[rows, :]), (th[...], tl[...]), ((1,), (0,)))
        for k in group:
            first_row = IMAGE_STARTS[k] - at
            share = 0.5 if IMAGE_SIZES[k] == 32 else 1.0
            emit(outs[k], terms[first_row : first_row + IMAGE_SIZES[k], :], share * sums)
    outs = outs[len(image_pieces) :]
    for group in ((0, 1), (2, 3, 4)):
        at = TEXT_STARTS[group[0]]
        cols = slice(at, at + sum(TEXT_SIZES[k] for k in group))
        terms = dot3((wh[:, cols], wl[:, cols]), (ih[...], il[...]), ((0,), (0,)))
        for k in group:
            first_row = TEXT_STARTS[k] - at
            outs[k][...] = terms[first_row : first_row + TEXT_SIZES[k], :]


def visit(image_pieces, text_pieces, *refs):
    log_scale_ref, bias_ref, place_ref = refs[:3]
    refs = refs[3:]
    image_refs = refs[:N_IMAGE]
    text_refs = refs[N_IMAGE : N_IMAGE + N_TEXT]
    sums_ref, *outs, ih, il, th, tl, wh, wl, irow, trow = refs[N_IMAGE + N_TEXT :]
    fill(image_refs, IMAGE_PARTS, ih, il, irow)
    fill(text_refs, TEXT_PARTS, th, tl, trow)
    scale = jnp.exp(log_scale_ref[...])
    offset = bias_ref[...]
    tags = jnp.transpose(jnp.broadcast_to(irow[0:1, :], (128, SIDE)))
    text_tags = trow[0:1, :]
    losses_sum = jnp.zeros((8, 128), F32)
    moment_sum = jnp.zeros((8, 128), F32)
    slope_sum = jnp.zeros((8, 128), F32)

    def fold(v):
        return jnp.sum(v.reshape(CHUNK // 8, 8, 128), axis=0)

    for k in range(SIDE // CHUNK):
        rows = slice(k * CHUNK, (k + 1) * CHUNK)
        dots = dot3((ih[rows, :], il[rows, :]), (th[...], tl[...]), ((1,), (1,)))
        for j in range(SIDE // 128):
            lanes = slice(128 * j, 128 * j + 128)
            moved = scale * dots[:, lanes]
            logits = moved + offset
            same = tags[rows, :] == text_tags[:, lanes]
            v = jnp.where(same, -logits, logits)
            e = jnp.exp(-jnp.abs(v))
            u = 1.0 + e
            r = 1.0 / u
            losses = jnp.maximum(v, 0.0) + (jnp.log(u) + (e - (u - 1.0)) * r)
            sig = jnp.where(v >= 0.0, r, e * r)
            slope = jnp.where(same, -sig, sig)
            losses_sum += fold(losses)
            moment_sum += fold(slope * moved)
            slope_sum += fold(slope)
            a, b = split(scale * slope)
            wh[rows, lanes] = a
            wl[rows, lanes] = b
    row = lax.broadcasted_iota(jnp.int32, (8, 128), 0)
    lane = lax.broadcasted_iota(jnp.int32, (8, 128), 1)
    mine = lane + 128 * (row % 2) == place_ref[...]
    sums = jnp.zeros((8, 128), F32)
    for k, total in enumerate((losses_sum, moment_sum, slope_sum)):
        sums = jnp.where(mine & (row // 2 == k), jnp.sum(total, keepdims=True), sums)
    sums_ref[...] = sums
    gradients(image_pieces, text_pieces, (ih, il, th, tl, wh, wl), sums, outs)


def unpack(kept_ref, came_ref, other_ref, rows_out, sums_out):
    for r in range(ROWS // 8):
        for c in range(COLS):
            at = r * COLS + c
            rows_out[8 * r : 8 * r + 8, 128 * c : 128 * c + 128] = kept_ref[at] + came_ref[at] + other_ref[1 + at]
    sums_out[...] = kept_ref[MSG - 1] + came_ref[MSG - 1] + other_ref[0]


def tiles(count):
    return jax.ShapeDtypeStruct((count, 8, 128), F32)


def rows_of(count):
    return jax.ShapeDtypeStruct((count, D), F32)


def vmem(count):
    return [pl.BlockSpec(memory_space=pltpu.VMEM)] * count


def cost(products, operands):
    return pl.CostEstimate(flops=6 * products, bytes_accessed=operands, transcendentals=0)


def shapes_of(image_pieces, text_pieces):
    return tuple(tiles(IMAGE_SIZES[k] // 8 * COLS + 1) for k in image_pieces) + tuple(
        rows_of(TEXT_SIZES[k]) for k in text_pieces
    )


def put(block, top, bottom):
    return jnp.pad(block, ((top, bottom),) + ((0, 0),) * (block.ndim - 1))


def shards(image, text, image_ids, text_ids, log_scale, bias):
    i0, t0 = pl.pallas_call(
        pack,
        out_shape=(tiles(MSG), tiles(MSG)),
        in_specs=vmem(4),
        out_specs=tuple(vmem(2)),
    )(image, text, image_ids.reshape(1, ROWS), text_ids.reshape(1, ROWS))

    c0 = jnp.concatenate([i0, send(i0, SWAP)], axis=0)
    z1 = send(c0, along_z(1))
    a = send(t0, first(1))
    b = send(t0, first(-1))
    c = send(t0, first(2))
    y0 = jnp.concatenate([t0, a, b, c], axis=0)
    z2 = send(z1, along_z(1))
    s1 = send(z1, SWAP)
    yp = send(y0, second(1))
    ym = send(y0, second(-1))
    z3 = send(z2, along_z(1))
    s2 = send(z2, SWAP)
    y2a = send(yp[: 2 * MSG], second(1))
    y2b = send(ym[2 * MSG :], second(-1))
    z4 = send(z3[:MSG], along_z(1))
    s3 = send(z3, SWAP)
    s4 = send(z4, SWAP)

    early = shapes_of(PIECES, range(N_TEXT))
    place = lax.axis_index("blk") * 4 + lax.axis_index("group")
    *_, gc, g1, g2, g3, g4, h1, h2, h3, h4, k0, kp, km, k2a, k2b = pl.pallas_call(
        lambda *refs: visit(PIECES, range(N_TEXT), *refs),
        out_shape=(jax.ShapeDtypeStruct((8, 128), F32),) + early,
        in_specs=vmem(3 + N_IMAGE + N_TEXT),
        out_specs=tuple(vmem(1 + len(early))),
        scratch_shapes=[pltpu.VMEM((SIDE, D), BF16)] * 4
        + [pltpu.VMEM((SIDE, SIDE), BF16)] * 2
        + [pltpu.VMEM((8, SIDE), F32)] * 2,
        compiler_params=pltpu.CompilerParams(vmem_limit_bytes=40 * 2**20),
        cost_estimate=cost(3 * SIDE * SIDE * D, 8 * SIDE * D),
    )(
        log_scale.reshape(1, 1), bias.reshape(1, 1), place.reshape(1, 1),
        c0, z1, z2, z3, z4, s1, s2, s3, s4,
        y0, yp, ym, y2a, y2b,
    )

    q4 = send(h4, SWAP)
    r2a = send(k2a, second(-1))
    r2b = send(k2b, second(1))
    w4 = send(g4 + q4, along_z(-1))
    q3 = send(h3, SWAP)
    w3 = send(g3 + q3 + put(w4, 0, MSG - 1), along_z(-1))
    rp = send(kp + put(r2a, 0, 64), second(-1))
    rm = send(km + put(r2b, 64, 0), second(1))
    q2 = send(h2, SWAP)
    q1 = send(h1, SWAP)
    w2 = send(g2 + q2 + w3, along_z(-1))
    w1 = send(g1 + q1 + w2, along_z(-1))
    k0 = k0 + rp + rm
    ra = send(k0[32:64], first(-1))
    rb = send(k0[64:96], first(1))
    rc = send(k0[96:128], first(2))
    grad_text = k0[:32] + ra + rb + rc
    other = send(gc[MSG - 1 :] + w1[MSG - 1 :], SWAP)
    grad_image, sums = pl.pallas_call(
        unpack,
        out_shape=(rows_of(ROWS), jax.ShapeDtypeStruct((8, 128), F32)),
        in_specs=vmem(3),
        out_specs=tuple(vmem(2)),
        compiler_params=pltpu.CompilerParams(vmem_limit_bytes=2 * 2**20),
    )(gc, w1, other)
    for route in (first, second):
        sums = (sums + send(sums, route(2))) + (send(sums, route(1)) + send(sums, route(-1)))
    statistics = jnp.sum(sums[:6].reshape(3, 256), axis=1) * (2.0**-26)
    return grad_image, grad_text, statistics


def solution(mesh):
    rows, ids = P(AXES, None), P(AXES)
    return jax.shard_map(
        shards,
        mesh=mesh,
        in_specs=(rows, rows, ids, ids, P(), P()),
        out_specs=(rows, rows, P()),
        check_vma=False,
    )
```

```python
import jax
import jax.numpy as jnp
from jax import lax
from jax.experimental import pallas as pl
from jax.experimental.pallas import tpu as pltpu
from jax.sharding import PartitionSpec as P

AXES = ("blk", "group")
NX, NY, NZ = 4, 4, 8
ROWS, D = 32, 1152
COLS = D // 128
MSG = ROWS // 8 * COLS + 1
HALF = ROWS // 16 * COLS
SIDE = 512
F32, BF16 = jnp.float32, jnp.bfloat16


def spot(x, y, z, c):
    return (((x % 2) * NY + y) * NZ + z) * 4 + (x // 2) * 2 + c


def table(move):
    pairs = []
    for x in range(NX):
        for y in range(NY):
            for z in range(NZ):
                for c in range(2):
                    a, b, d, e = move(x, y, z, c)
                    pairs.append((spot(x, y, z, c), spot(a % NX, b % NY, d % NZ, e)))
    return pairs


SWAP = table(lambda x, y, z, c: (x, y, z, 1 - c))


def along_z(way):
    return table(lambda x, y, z, c: (x, y, z + (way if c == 0 else -way), c))


def first(way):
    return table(lambda x, y, z, c: (x + way, y, z, c) if c == 0 else (x, y + way, z, c))


def second(way):
    return table(lambda x, y, z, c: (x, y + way, z, c) if c == 0 else (x + way, y, z, c))


def send(block, route):
    return lax.ppermute(block, AXES, route)


def pack(image_ref, text_ref, image_ids_ref, text_ids_ref, image_out, text_out):
    for rows, ids, out in ((image_ref, image_ids_ref, image_out), (text_ref, text_ids_ref, text_out)):
        for r in range(ROWS // 8):
            for c in range(COLS):
                at = r * COLS + c
                out[at + (1 if at >= HALF else 0)] = rows[8 * r : 8 * r + 8, 128 * c : 128 * c + 128]
        out[HALF] = jnp.zeros((8, 128), F32)
        out[HALF, 0:1, 0:ROWS] = ids[...].astype(F32)


def whole(operand, block):
    at = block * MSG
    return [(operand, at, at + HALF, 0, 16), (operand, at + HALF + 1, at + HALF, 16, 16)]


IMAGE_SIZES = (64, 64, 64, 64, 32, 64, 64, 64, 32)
TEXT_SIZES = (128, 128, 128, 64, 64)
IMAGE_PARTS = [part for k, size in enumerate(IMAGE_SIZES) for b in range(size // 32) for part in whole(k, b)]
TEXT_PARTS = [part for k, size in enumerate(TEXT_SIZES) for b in range(size // 32) for part in whole(k, b)]
IMAGE_STARTS = tuple(sum(IMAGE_SIZES[:k]) for k in range(len(IMAGE_SIZES)))
TEXT_STARTS = tuple(sum(TEXT_SIZES[:k]) for k in range(len(TEXT_SIZES)))
PIECES = range(len(IMAGE_SIZES))
N_IMAGE, N_TEXT = len(IMAGE_SIZES), len(TEXT_SIZES)


def split(value):
    high = value.astype(BF16)
    return high, (value - high.astype(F32)).astype(BF16)


def fill(refs, parts, high, low, row):
    start = 0
    for operand, at, tag, lane, rows in parts:
        ref = refs[operand]
        for c in range(COLS):
            piece = jnp.concatenate([ref[at + c], ref[at + COLS + c]], axis=0)
            a, b = split(piece)
            high[start : start + 16, 128 * c : 128 * c + 128] = a
            low[start : start + 16, 128 * c : 128 * c + 128] = b
        row[0:1, start : start + rows] = ref[tag, 0:1, lane : lane + rows]
        start += rows


def dot3(a, b, dims):
    def one(p, q):
        return lax.dot_general(p, q, (dims, ((), ())), preferred_element_type=F32)

    return one(a[0], b[0]) + (one(a[0], b[1]) + one(a[1], b[0]))


CHUNK = 256


def emit(out, rows, sums):
    for r in range(rows.shape[0] // 8):
        for c in range(COLS):
            at = r * COLS + c
            out[at + (1 if r >= ROWS // 8 else 0)] = rows[8 * r : 8 * r + 8, 128 * c : 128 * c + 128]
    out[MSG - 1] = sums


def gradients(image_pieces, text_pieces, held, sums, outs):
    ih, il, th, tl, wh, wl = held
    for group in ((0, 1, 2, 3), (4, 5, 6, 7, 8)):
        at = IMAGE_STARTS[group[0]]
        rows = slice(at, at + sum(IMAGE_SIZES[k] for k in group))
        terms = dot3((wh[rows, :], wl[rows, :]), (th[...], tl[...]), ((1,), (0,)))
        for k in group:
            first_row = IMAGE_STARTS[k] - at
            share = 0.5 if IMAGE_SIZES[k] == 32 else 1.0
            emit(outs[k], terms[first_row : first_row + IMAGE_SIZES[k], :], share * sums)
    outs = outs[len(image_pieces) :]
    for group in ((0, 1), (2, 3, 4)):
        at = TEXT_STARTS[group[0]]
        cols = slice(at, at + sum(TEXT_SIZES[k] for k in group))
        terms = dot3((wh[:, cols], wl[:, cols]), (ih[...], il[...]), ((0,), (0,)))
        for k in group:
            first_row = TEXT_STARTS[k] - at
            outs[k][...] = terms[first_row : first_row + TEXT_SIZES[k], :]


def visit(image_pieces, text_pieces, *refs):
    log_scale_ref, bias_ref, place_ref = refs[:3]
    refs = refs[3:]
    image_refs = refs[:N_IMAGE]
    text_refs = refs[N_IMAGE : N_IMAGE + N_TEXT]
    sums_ref, *outs, ih, il, th, tl, wh, wl, irow, trow = refs[N_IMAGE + N_TEXT :]
    fill(image_refs, IMAGE_PARTS, ih, il, irow)
    fill(text_refs, TEXT_PARTS, th, tl, trow)
    scale = jnp.exp(log_scale_ref[...])
    offset = bias_ref[...]
    tags = jnp.transpose(jnp.broadcast_to(irow[0:1, :], (128, SIDE)))
    text_tags = trow[0:1, :]
    losses_sum = jnp.zeros((8, 128), F32)
    moment_sum = jnp.zeros((8, 128), F32)
    slope_sum = jnp.zeros((8, 128), F32)

    def fold(v):
        return jnp.sum(v.reshape(CHUNK // 8, 8, 128), axis=0)

    for k in range(SIDE // CHUNK):
        rows = slice(k * CHUNK, (k + 1) * CHUNK)
        dots = dot3((ih[rows, :], il[rows, :]), (th[...], tl[...]), ((1,), (1,)))
        for j in range(SIDE // 128):
            lanes = slice(128 * j, 128 * j + 128)
            moved = scale * dots[:, lanes]
            logits = moved + offset
            same = tags[rows, :] == text_tags[:, lanes]
            v = jnp.where(same, -logits, logits)
            e = jnp.exp(-jnp.abs(v))
            u = 1.0 + e
            r = 1.0 / u
            losses = jnp.maximum(v, 0.0) + (jnp.log(u) + (e - (u - 1.0)) * r)
            sig = jnp.where(v >= 0.0, r, e * r)
            slope = jnp.where(same, -sig, sig)
            losses_sum += fold(losses)
            moment_sum += fold(slope * moved)
            slope_sum += fold(slope)
            a, b = split(scale * slope)
            wh[rows, lanes] = a
            wl[rows, lanes] = b
    row = lax.broadcasted_iota(jnp.int32, (8, 128), 0)
    lane = lax.broadcasted_iota(jnp.int32, (8, 128), 1)
    mine = lane + 128 * (row % 2) == place_ref[...]
    sums = jnp.zeros((8, 128), F32)
    for k, total in enumerate((losses_sum, moment_sum, slope_sum)):
        sums = jnp.where(mine & (row // 2 == k), jnp.sum(total, keepdims=True), sums)
    sums_ref[...] = sums
    gradients(image_pieces, text_pieces, (ih, il, th, tl, wh, wl), sums, outs)


def unpack(kept_ref, came_ref, other_ref, rows_out, sums_out):
    for r in range(ROWS // 8):
        for c in range(COLS):
            at = r * COLS + c
            rows_out[8 * r : 8 * r + 8, 128 * c : 128 * c + 128] = kept_ref[at] + came_ref[at] + other_ref[1 + at]
    sums_out[...] = kept_ref[MSG - 1] + came_ref[MSG - 1] + other_ref[0]


def tiles(count):
    return jax.ShapeDtypeStruct((count, 8, 128), F32)


def rows_of(count):
    return jax.ShapeDtypeStruct((count, D), F32)


def vmem(count):
    return [pl.BlockSpec(memory_space=pltpu.VMEM)] * count


def cost(products, operands):
    return pl.CostEstimate(flops=6 * products, bytes_accessed=operands, transcendentals=0)


def shapes_of(image_pieces, text_pieces):
    return tuple(tiles(IMAGE_SIZES[k] // 8 * COLS + 1) for k in image_pieces) + tuple(
        rows_of(TEXT_SIZES[k]) for k in text_pieces
    )


def behind(first_block, *blocks):
    anywhere = pl.BlockSpec(memory_space=pl.ANY)
    return pl.pallas_call(
        lambda *refs: None,
        out_shape=tuple(jax.ShapeDtypeStruct(block.shape, block.dtype) for block in blocks),
        in_specs=[anywhere] * (1 + len(blocks)),
        out_specs=(anywhere,) * len(blocks),
        input_output_aliases={1 + n: n for n in range(len(blocks))},
        compiler_params=pltpu.CompilerParams(vmem_limit_bytes=2**20),
    )(first_block, *blocks)


def put(block, top, bottom):
    return jnp.pad(block, ((top, bottom),) + ((0, 0),) * (block.ndim - 1))


def shards(image, text, image_ids, text_ids, log_scale, bias):
    i0, t0 = pl.pallas_call(
        pack,
        out_shape=(tiles(MSG), tiles(MSG)),
        in_specs=vmem(4),
        out_specs=tuple(vmem(2)),
    )(image, text, image_ids.reshape(1, ROWS), text_ids.reshape(1, ROWS))

    c0 = jnp.concatenate([i0, send(i0, SWAP)], axis=0)
    z1 = send(c0, along_z(1))
    a = send(t0, first(1))
    b = send(t0, first(-1))
    c = send(t0, first(2))
    y0 = jnp.concatenate([t0, a, b, c], axis=0)
    z2 = send(z1, along_z(1))
    s1 = send(z1, SWAP)
    yp = send(y0, second(1))
    ym = send(y0, second(-1))
    z3 = send(z2, along_z(1))
    s2 = send(z2, SWAP)
    y2a = send(yp[: 2 * MSG], second(1))
    y2b = send(ym[2 * MSG :], second(-1))
    z4 = send(z3[:MSG], along_z(1))
    s3 = send(z3, SWAP)
    s4 = send(z4, SWAP)

    early = shapes_of(PIECES, range(N_TEXT))
    place = lax.axis_index("blk") * 4 + lax.axis_index("group")
    *_, gc, g1, g2, g3, g4, h1, h2, h3, h4, k0, kp, km, k2a, k2b = pl.pallas_call(
        lambda *refs: visit(PIECES, range(N_TEXT), *refs),
        out_shape=(jax.ShapeDtypeStruct((8, 128), F32),) + early,
        in_specs=vmem(3 + N_IMAGE + N_TEXT),
        out_specs=tuple(vmem(1 + len(early))),
        scratch_shapes=[pltpu.VMEM((SIDE, D), BF16)] * 4
        + [pltpu.VMEM((SIDE, SIDE), BF16)] * 2
        + [pltpu.VMEM((8, SIDE), F32)] * 2,
        compiler_params=pltpu.CompilerParams(vmem_limit_bytes=40 * 2**20),
        cost_estimate=cost(3 * SIDE * SIDE * D, 8 * SIDE * D),
    )(
        log_scale.reshape(1, 1), bias.reshape(1, 1), place.reshape(1, 1),
        c0, z1, z2, z3, z4, s1, s2, s3, s4,
        y0, yp, ym, y2a, y2b,
    )

    q4 = send(h4, SWAP)
    g4 = g4 + q4
    w4 = send(g4, along_z(-1))
    k2a, k2b = behind(g4, k2a, k2b)
    r2a = send(k2a, second(-1))
    r2b = send(k2b, second(1))
    q3 = send(h3, SWAP)
    w3 = send(g3 + q3 + put(w4, 0, MSG - 1), along_z(-1))
    rp = send(kp + put(r2a, 0, 64), second(-1))
    rm = send(km + put(r2b, 64, 0), second(1))
    q2 = send(h2, SWAP)
    q1 = send(h1, SWAP)
    w2 = send(g2 + q2 + w3, along_z(-1))
    w1 = send(g1 + q1 + w2, along_z(-1))
    k0 = k0 + rp + rm
    other = send(gc[MSG - 1 :] + w1[MSG - 1 :], SWAP)
    grad_image, sums = pl.pallas_call(
        unpack,
        out_shape=(rows_of(ROWS), jax.ShapeDtypeStruct((8, 128), F32)),
        in_specs=vmem(3),
        out_specs=tuple(vmem(2)),
        compiler_params=pltpu.CompilerParams(vmem_limit_bytes=2 * 2**20),
    )(gc, w1, other)
    (k0,) = behind(sums, k0)
    ra = send(k0[32:64], first(-1))
    rb = send(k0[64:96], first(1))
    rc = send(k0[96:128], first(2))
    grad_text = k0[:32] + ra + rb + rc
    lines = [[spot(x, y, z, c) for x in range(NX) for y in range(NY)] for z in range(NZ) for c in range(2)]
    every = lax.all_to_all(
        jnp.broadcast_to(sums, (NX * NY, 8, 128)), AXES, 0, 0, axis_index_groups=lines, tiled=True
    )
    statistics = jnp.sum(every[:, :6].reshape(NX * NY, 3, 256), axis=(0, 2)) * (2.0**-26)
    return grad_image, grad_text, statistics


def solution(mesh):
    rows, ids = P(AXES, None), P(AXES)
    return jax.shard_map(
        shards,
        mesh=mesh,
        in_specs=(rows, rows, ids, ids, P(), P()),
        out_specs=(rows, rows, P()),
        check_vma=False,
    )
```

```python
import jax
import jax.numpy as jnp
from jax import lax
from jax.experimental import pallas as pl
from jax.experimental.pallas import tpu as pltpu
from jax.sharding import PartitionSpec as P

AXES = ("blk", "group")
NX, NY, NZ = 4, 4, 8
ROWS, D = 32, 1152
COLS = D // 128
MSG = ROWS // 8 * COLS + 1
HALF = ROWS // 16 * COLS
SIDE = 512
F32, BF16 = jnp.float32, jnp.bfloat16


def spot(x, y, z, c):
    return (((x % 2) * NY + y) * NZ + z) * 4 + (x // 2) * 2 + c


def table(move):
    pairs = []
    for x in range(NX):
        for y in range(NY):
            for z in range(NZ):
                for c in range(2):
                    a, b, d, e = move(x, y, z, c)
                    pairs.append((spot(x, y, z, c), spot(a % NX, b % NY, d % NZ, e)))
    return pairs


SWAP = table(lambda x, y, z, c: (x, y, z, 1 - c))


def along_z(way):
    return table(lambda x, y, z, c: (x, y, z + (way if c == 0 else -way), c))


def first(way):
    return table(lambda x, y, z, c: (x + way, y, z, c) if c == 0 else (x, y + way, z, c))


def second(way):
    return table(lambda x, y, z, c: (x, y + way, z, c) if c == 0 else (x + way, y, z, c))


def send(block, route):
    return lax.ppermute(block, AXES, route)


def pack(image_ref, text_ref, image_ids_ref, text_ids_ref, image_out, text_out):
    for rows, ids, out in ((image_ref, image_ids_ref, image_out), (text_ref, text_ids_ref, text_out)):
        for r in range(ROWS // 8):
            for c in range(COLS):
                at = r * COLS + c
                out[at + (1 if at >= HALF else 0)] = rows[8 * r : 8 * r + 8, 128 * c : 128 * c + 128]
        out[HALF] = jnp.zeros((8, 128), F32)
        out[HALF, 0:1, 0:ROWS] = ids[...].astype(F32)


def whole(operand, block):
    at = block * MSG
    return [(operand, at, at + HALF, 0, 16), (operand, at + HALF + 1, at + HALF, 16, 16)]


IMAGE_SIZES = (64, 64, 64, 64, 32, 64, 64, 64, 32)
TEXT_SIZES = (128, 128, 128, 64, 64)
IMAGE_PARTS = [part for k, size in enumerate(IMAGE_SIZES) for b in range(size // 32) for part in whole(k, b)]
TEXT_PARTS = [part for k, size in enumerate(TEXT_SIZES) for b in range(size // 32) for part in whole(k, b)]
IMAGE_STARTS = tuple(sum(IMAGE_SIZES[:k]) for k in range(len(IMAGE_SIZES)))
TEXT_STARTS = tuple(sum(TEXT_SIZES[:k]) for k in range(len(TEXT_SIZES)))
PIECES = range(len(IMAGE_SIZES))
N_IMAGE, N_TEXT = len(IMAGE_SIZES), len(TEXT_SIZES)


def split(value):
    high = value.astype(BF16)
    return high, (value - high.astype(F32)).astype(BF16)


def fill(refs, parts, high, low, row):
    start = 0
    for operand, at, tag, lane, rows in parts:
        ref = refs[operand]
        for c in range(COLS):
            piece = jnp.concatenate([ref[at + c], ref[at + COLS + c]], axis=0)
            a, b = split(piece)
            high[start : start + 16, 128 * c : 128 * c + 128] = a
            low[start : start + 16, 128 * c : 128 * c + 128] = b
        row[0:1, start : start + rows] = ref[tag, 0:1, lane : lane + rows]
        start += rows


def dot3(a, b, dims):
    def one(p, q):
        return lax.dot_general(p, q, (dims, ((), ())), preferred_element_type=F32)

    return one(a[0], b[0]) + (one(a[0], b[1]) + one(a[1], b[0]))


CHUNK = 256


def emit(out, rows, sums):
    for r in range(rows.shape[0] // 8):
        for c in range(COLS):
            at = r * COLS + c
            out[at + (1 if r >= ROWS // 8 else 0)] = rows[8 * r : 8 * r + 8, 128 * c : 128 * c + 128]
    out[MSG - 1] = sums


def gradients(image_pieces, text_pieces, held, sums, outs):
    ih, il, th, tl, wh, wl = held
    for group in ((0, 1, 2, 3), (4, 5, 6, 7, 8)):
        at = IMAGE_STARTS[group[0]]
        rows = slice(at, at + sum(IMAGE_SIZES[k] for k in group))
        terms = dot3((wh[rows, :], wl[rows, :]), (th[...], tl[...]), ((1,), (0,)))
        for k in group:
            first_row = IMAGE_STARTS[k] - at
            share = 0.5 if IMAGE_SIZES[k] == 32 else 1.0
            emit(outs[k], terms[first_row : first_row + IMAGE_SIZES[k], :], share * sums)
    outs = outs[len(image_pieces) :]
    for group in ((0, 1), (2, 3, 4)):
        at = TEXT_STARTS[group[0]]
        cols = slice(at, at + sum(TEXT_SIZES[k] for k in group))
        terms = dot3((wh[:, cols], wl[:, cols]), (ih[...], il[...]), ((0,), (0,)))
        for k in group:
            first_row = TEXT_STARTS[k] - at
            outs[k][...] = terms[first_row : first_row + TEXT_SIZES[k], :]


def visit(image_pieces, text_pieces, *refs):
    log_scale_ref, bias_ref, place_ref = refs[:3]
    refs = refs[3:]
    image_refs = refs[:N_IMAGE]
    text_refs = refs[N_IMAGE : N_IMAGE + N_TEXT]
    sums_ref, *outs, ih, il, th, tl, wh, wl, irow, trow = refs[N_IMAGE + N_TEXT :]
    fill(image_refs, IMAGE_PARTS, ih, il, irow)
    fill(text_refs, TEXT_PARTS, th, tl, trow)
    scale = jnp.exp(log_scale_ref[...])
    offset = bias_ref[...]
    tags = jnp.transpose(jnp.broadcast_to(irow[0:1, :], (128, SIDE)))
    text_tags = trow[0:1, :]
    losses_sum = jnp.zeros((8, 128), F32)
    moment_sum = jnp.zeros((8, 128), F32)
    slope_sum = jnp.zeros((8, 128), F32)

    def fold(v):
        return jnp.sum(v.reshape(CHUNK // 8, 8, 128), axis=0)

    for k in range(SIDE // CHUNK):
        rows = slice(k * CHUNK, (k + 1) * CHUNK)
        dots = dot3((ih[rows, :], il[rows, :]), (th[...], tl[...]), ((1,), (1,)))
        for j in range(SIDE // 128):
            lanes = slice(128 * j, 128 * j + 128)
            moved = scale * dots[:, lanes]
            logits = moved + offset
            same = tags[rows, :] == text_tags[:, lanes]
            v = jnp.where(same, -logits, logits)
            e = jnp.exp(-jnp.abs(v))
            u = 1.0 + e
            r = 1.0 / u
            losses = jnp.maximum(v, 0.0) + (jnp.log(u) + (e - (u - 1.0)) * r)
            sig = jnp.where(v >= 0.0, r, e * r)
            slope = jnp.where(same, -sig, sig)
            losses_sum += fold(losses)
            moment_sum += fold(slope * moved)
            slope_sum += fold(slope)
            a, b = split(scale * slope)
            wh[rows, lanes] = a
            wl[rows, lanes] = b
    row = lax.broadcasted_iota(jnp.int32, (8, 128), 0)
    lane = lax.broadcasted_iota(jnp.int32, (8, 128), 1)
    mine = lane + 128 * (row % 2) == place_ref[...]
    sums = jnp.zeros((8, 128), F32)
    for k, total in enumerate((losses_sum, moment_sum, slope_sum)):
        sums = jnp.where(mine & (row // 2 == k), jnp.sum(total, keepdims=True), sums)
    sums_ref[...] = sums
    gradients(image_pieces, text_pieces, (ih, il, th, tl, wh, wl), sums, outs)


def unpack(kept_ref, came_ref, other_ref, after_ref, rows_out, sums_out):
    for r in range(ROWS // 8):
        for c in range(COLS):
            at = r * COLS + c
            rows_out[8 * r : 8 * r + 8, 128 * c : 128 * c + 128] = kept_ref[at] + came_ref[at] + other_ref[1 + at]
    sums_out[...] = kept_ref[MSG - 1] + came_ref[MSG - 1] + other_ref[0]


def tiles(count):
    return jax.ShapeDtypeStruct((count, 8, 128), F32)


def rows_of(count):
    return jax.ShapeDtypeStruct((count, D), F32)


def vmem(count):
    return [pl.BlockSpec(memory_space=pltpu.VMEM)] * count


def cost(products, operands):
    return pl.CostEstimate(flops=6 * products, bytes_accessed=operands, transcendentals=0)


def shapes_of(image_pieces, text_pieces):
    return tuple(tiles(IMAGE_SIZES[k] // 8 * COLS + 1) for k in image_pieces) + tuple(
        rows_of(TEXT_SIZES[k]) for k in text_pieces
    )


def behind(first_block, *blocks):
    anywhere = pl.BlockSpec(memory_space=pl.ANY)
    return pl.pallas_call(
        lambda *refs: None,
        out_shape=tuple(jax.ShapeDtypeStruct(block.shape, block.dtype) for block in blocks),
        in_specs=[anywhere] * (1 + len(blocks)),
        out_specs=(anywhere,) * len(blocks),
        input_output_aliases={1 + n: n for n in range(len(blocks))},
        compiler_params=pltpu.CompilerParams(vmem_limit_bytes=2**20),
    )(first_block, *blocks)


def put(block, top, bottom):
    return jnp.pad(block, ((top, bottom),) + ((0, 0),) * (block.ndim - 1))


def shards(image, text, image_ids, text_ids, log_scale, bias):
    i0, t0 = pl.pallas_call(
        pack,
        out_shape=(tiles(MSG), tiles(MSG)),
        in_specs=vmem(4),
        out_specs=tuple(vmem(2)),
    )(image, text, image_ids.reshape(1, ROWS), text_ids.reshape(1, ROWS))

    c0 = jnp.concatenate([i0, send(i0, SWAP)], axis=0)
    z1 = send(c0, along_z(1))
    a = send(t0, first(1))
    b = send(t0, first(-1))
    c = send(t0, first(2))
    y0 = jnp.concatenate([t0, a, b, c], axis=0)
    z2 = send(z1, along_z(1))
    s1 = send(z1, SWAP)
    yp = send(y0, second(1))
    ym = send(y0, second(-1))
    z3 = send(z2, along_z(1))
    s2 = send(z2, SWAP)
    y2a = send(yp[: 2 * MSG], second(1))
    y2b = send(ym[2 * MSG :], second(-1))
    z4 = send(z3[:MSG], along_z(1))
    s3 = send(z3, SWAP)
    s4 = send(z4, SWAP)

    early = shapes_of(PIECES, range(N_TEXT))
    place = lax.axis_index("blk") * 4 + lax.axis_index("group")
    *_, gc, g1, g2, g3, g4, h1, h2, h3, h4, k0, kp, km, k2a, k2b = pl.pallas_call(
        lambda *refs: visit(PIECES, range(N_TEXT), *refs),
        out_shape=(jax.ShapeDtypeStruct((8, 128), F32),) + early,
        in_specs=vmem(3 + N_IMAGE + N_TEXT),
        out_specs=tuple(vmem(1 + len(early))),
        scratch_shapes=[pltpu.VMEM((SIDE, D), BF16)] * 4
        + [pltpu.VMEM((SIDE, SIDE), BF16)] * 2
        + [pltpu.VMEM((8, SIDE), F32)] * 2,
        compiler_params=pltpu.CompilerParams(vmem_limit_bytes=40 * 2**20),
        cost_estimate=cost(3 * SIDE * SIDE * D, 8 * SIDE * D),
    )(
        log_scale.reshape(1, 1), bias.reshape(1, 1), place.reshape(1, 1),
        c0, z1, z2, z3, z4, s1, s2, s3, s4,
        y0, yp, ym, y2a, y2b,
    )

    q4 = send(h4, SWAP)
    g4 = g4 + q4
    w4 = send(g4, along_z(-1))
    k2a, k2b = behind(g4, k2a, k2b)
    r2a = send(k2a, second(-1))
    r2b = send(k2b, second(1))
    q3 = send(h3, SWAP)
    w3 = send(g3 + q3 + put(w4, 0, MSG - 1), along_z(-1))
    rp = send(kp + put(r2a, 0, 64), second(-1))
    rm = send(km + put(r2b, 64, 0), second(1))
    q2 = send(h2, SWAP)
    q1 = send(h1, SWAP)
    w2 = send(g2 + q2 + w3, along_z(-1))
    w1 = send(g1 + q1 + w2, along_z(-1))
    k0 = k0 + rp + rm
    ra = send(k0[32:64], first(-1))
    rb = send(k0[64:96], first(1))
    rc = send(k0[96:128], first(2))
    grad_text = k0[:32] + ra + rb + rc
    other = send(gc[MSG - 1 :] + w1[MSG - 1 :], SWAP)
    grad_image, sums = pl.pallas_call(
        unpack,
        out_shape=(rows_of(ROWS), jax.ShapeDtypeStruct((8, 128), F32)),
        in_specs=vmem(3) + [pl.BlockSpec(memory_space=pl.ANY)],
        out_specs=tuple(vmem(2)),
        compiler_params=pltpu.CompilerParams(vmem_limit_bytes=2 * 2**20),
    )(gc, w1, other, ra)
    lines = [[spot(x, y, z, c) for x in range(NX) for y in range(NY)] for z in range(NZ) for c in range(2)]
    every = lax.all_to_all(
        jnp.broadcast_to(sums, (NX * NY, 8, 128)), AXES, 0, 0, axis_index_groups=lines, tiled=True
    )
    statistics = jnp.sum(every[:, :6].reshape(NX * NY, 3, 256), axis=(0, 2)) * (2.0**-26)
    return grad_image, grad_text, statistics


def solution(mesh):
    rows, ids = P(AXES, None), P(AXES)
    return jax.shard_map(
        shards,
        mesh=mesh,
        in_specs=(rows, rows, ids, ids, P(), P()),
        out_specs=(rows, rows, P()),
        check_vma=False,
    )
```

```python
import jax
import jax.numpy as jnp
from jax import lax
from jax.experimental import pallas as pl
from jax.experimental.pallas import tpu as pltpu
from jax.sharding import PartitionSpec as P

AXES = ("blk", "group")
NX, NY, NZ = 4, 4, 8
ROWS, D = 32, 1152
COLS = D // 128
MSG = ROWS // 8 * COLS + 1
HALF = ROWS // 16 * COLS
SIDE = 512
F32, BF16 = jnp.float32, jnp.bfloat16


def spot(x, y, z, c):
    return (((x % 2) * NY + y) * NZ + z) * 4 + (x // 2) * 2 + c


def table(move):
    pairs = []
    for x in range(NX):
        for y in range(NY):
            for z in range(NZ):
                for c in range(2):
                    a, b, d, e = move(x, y, z, c)
                    pairs.append((spot(x, y, z, c), spot(a % NX, b % NY, d % NZ, e)))
    return pairs


SWAP = table(lambda x, y, z, c: (x, y, z, 1 - c))


def along_z(way):
    return table(lambda x, y, z, c: (x, y, z + (way if c == 0 else -way), c))


def first(way):
    return table(lambda x, y, z, c: (x + way, y, z, c) if c == 0 else (x, y + way, z, c))


def second(way):
    return table(lambda x, y, z, c: (x, y + way, z, c) if c == 0 else (x + way, y, z, c))


def send(block, route):
    return lax.ppermute(block, AXES, route)


def pack(image_ref, text_ref, image_ids_ref, text_ids_ref, image_out, text_out):
    for rows, ids, out in ((image_ref, image_ids_ref, image_out), (text_ref, text_ids_ref, text_out)):
        for r in range(ROWS // 8):
            for c in range(COLS):
                at = r * COLS + c
                out[at + (1 if at >= HALF else 0)] = rows[8 * r : 8 * r + 8, 128 * c : 128 * c + 128]
        out[HALF] = jnp.zeros((8, 128), F32)
        out[HALF, 0:1, 0:ROWS] = ids[...].astype(F32)


def whole(operand, block):
    at = block * MSG
    return [(operand, at, at + HALF, 0, 16), (operand, at + HALF + 1, at + HALF, 16, 16)]


IMAGE_SIZES = (64, 64, 64, 64, 32, 64, 64, 64, 32)
TEXT_SIZES = (128, 128, 128, 64, 64)
IMAGE_PARTS = [part for k, size in enumerate(IMAGE_SIZES) for b in range(size // 32) for part in whole(k, b)]
TEXT_PARTS = [part for k, size in enumerate(TEXT_SIZES) for b in range(size // 32) for part in whole(k, b)]
IMAGE_STARTS = tuple(sum(IMAGE_SIZES[:k]) for k in range(len(IMAGE_SIZES)))
TEXT_STARTS = tuple(sum(TEXT_SIZES[:k]) for k in range(len(TEXT_SIZES)))
PIECES = range(len(IMAGE_SIZES))
N_IMAGE, N_TEXT = len(IMAGE_SIZES), len(TEXT_SIZES)


def split(value):
    high = value.astype(BF16)
    return high, (value - high.astype(F32)).astype(BF16)


def fill(refs, parts, high, low, row):
    start = 0
    for operand, at, tag, lane, rows in parts:
        ref = refs[operand]
        for c in range(COLS):
            piece = jnp.concatenate([ref[at + c], ref[at + COLS + c]], axis=0)
            a, b = split(piece)
            high[start : start + 16, 128 * c : 128 * c + 128] = a
            low[start : start + 16, 128 * c : 128 * c + 128] = b
        row[0:1, start : start + rows] = ref[tag, 0:1, lane : lane + rows]
        start += rows


def dot3(a, b, dims):
    def one(p, q):
        return lax.dot_general(p, q, (dims, ((), ())), preferred_element_type=F32)

    return one(a[0], b[0]) + (one(a[0], b[1]) + one(a[1], b[0]))


CHUNK = 256


def emit(out, rows, sums):
    for r in range(rows.shape[0] // 8):
        for c in range(COLS):
            at = r * COLS + c
            out[at + (1 if r >= ROWS // 8 else 0)] = rows[8 * r : 8 * r + 8, 128 * c : 128 * c + 128]
    out[MSG - 1] = sums


def gradients(image_pieces, text_pieces, held, sums, outs):
    ih, il, th, tl, wh, wl = held
    for group in ((0, 1, 2, 3), (4, 5, 6, 7, 8)):
        at = IMAGE_STARTS[group[0]]
        rows = slice(at, at + sum(IMAGE_SIZES[k] for k in group))
        terms = dot3((wh[rows, :], wl[rows, :]), (th[...], tl[...]), ((1,), (0,)))
        for k in group:
            first_row = IMAGE_STARTS[k] - at
            share = 0.5 if IMAGE_SIZES[k] == 32 else 1.0
            emit(outs[k], terms[first_row : first_row + IMAGE_SIZES[k], :], share * sums)
    outs = outs[len(image_pieces) :]
    for group in ((0, 1), (2, 3, 4)):
        at = TEXT_STARTS[group[0]]
        cols = slice(at, at + sum(TEXT_SIZES[k] for k in group))
        terms = dot3((wh[:, cols], wl[:, cols]), (ih[...], il[...]), ((0,), (0,)))
        for k in group:
            first_row = TEXT_STARTS[k] - at
            outs[k][...] = terms[first_row : first_row + TEXT_SIZES[k], :]


def visit(image_pieces, text_pieces, *refs):
    log_scale_ref, bias_ref, place_ref = refs[:3]
    refs = refs[3:]
    image_refs = refs[:N_IMAGE]
    text_refs = refs[N_IMAGE : N_IMAGE + N_TEXT]
    sums_ref, *outs, ih, il, th, tl, wh, wl, irow, trow = refs[N_IMAGE + N_TEXT :]
    fill(image_refs, IMAGE_PARTS, ih, il, irow)
    fill(text_refs, TEXT_PARTS, th, tl, trow)
    scale = jnp.exp(log_scale_ref[...])
    offset = bias_ref[...]
    tags = jnp.transpose(jnp.broadcast_to(irow[0:1, :], (128, SIDE)))
    text_tags = trow[0:1, :]
    losses_sum = jnp.zeros((8, 128), F32)
    moment_sum = jnp.zeros((8, 128), F32)
    slope_sum = jnp.zeros((8, 128), F32)

    def fold(v):
        return jnp.sum(v.reshape(CHUNK // 8, 8, 128), axis=0)

    for k in range(SIDE // CHUNK):
        rows = slice(k * CHUNK, (k + 1) * CHUNK)
        dots = dot3((ih[rows, :], il[rows, :]), (th[...], tl[...]), ((1,), (1,)))
        for j in range(SIDE // 128):
            lanes = slice(128 * j, 128 * j + 128)
            moved = scale * dots[:, lanes]
            logits = moved + offset
            same = tags[rows, :] == text_tags[:, lanes]
            v = jnp.where(same, -logits, logits)
            e = jnp.exp(-jnp.abs(v))
            u = 1.0 + e
            r = 1.0 / u
            losses = jnp.maximum(v, 0.0) + (jnp.log(u) + (e - (u - 1.0)) * r)
            sig = jnp.where(v >= 0.0, r, e * r)
            slope = jnp.where(same, -sig, sig)
            losses_sum += fold(losses)
            moment_sum += fold(slope * moved)
            slope_sum += fold(slope)
            a, b = split(scale * slope)
            wh[rows, lanes] = a
            wl[rows, lanes] = b
    row = lax.broadcasted_iota(jnp.int32, (8, 128), 0)
    lane = lax.broadcasted_iota(jnp.int32, (8, 128), 1)
    mine = lane + 128 * (row % 2) == place_ref[...]
    sums = jnp.zeros((8, 128), F32)
    for k, total in enumerate((losses_sum, moment_sum, slope_sum)):
        sums = jnp.where(mine & (row // 2 == k), jnp.sum(total, keepdims=True), sums)
    sums_ref[...] = sums
    gradients(image_pieces, text_pieces, (ih, il, th, tl, wh, wl), sums, outs)


def unpack(kept_ref, came_ref, other_ref, rows_out, sums_out):
    for r in range(ROWS // 8):
        for c in range(COLS):
            at = r * COLS + c
            rows_out[8 * r : 8 * r + 8, 128 * c : 128 * c + 128] = kept_ref[at] + came_ref[at] + other_ref[1 + at]
    sums_out[...] = kept_ref[MSG - 1] + came_ref[MSG - 1] + other_ref[0]


def tiles(count):
    return jax.ShapeDtypeStruct((count, 8, 128), F32)


def rows_of(count):
    return jax.ShapeDtypeStruct((count, D), F32)


def vmem(count):
    return [pl.BlockSpec(memory_space=pltpu.VMEM)] * count


def cost(products, operands):
    return pl.CostEstimate(flops=6 * products, bytes_accessed=operands, transcendentals=0)


def shapes_of(image_pieces, text_pieces):
    return tuple(tiles(IMAGE_SIZES[k] // 8 * COLS + 1) for k in image_pieces) + tuple(
        rows_of(TEXT_SIZES[k]) for k in text_pieces
    )


def behind(first_block, *blocks):
    anywhere = pl.BlockSpec(memory_space=pl.ANY)
    return pl.pallas_call(
        lambda *refs: None,
        out_shape=tuple(jax.ShapeDtypeStruct(block.shape, block.dtype) for block in blocks),
        in_specs=[anywhere] * (1 + len(blocks)),
        out_specs=(anywhere,) * len(blocks),
        input_output_aliases={1 + n: n for n in range(len(blocks))},
        compiler_params=pltpu.CompilerParams(vmem_limit_bytes=2**20),
    )(first_block, *blocks)


def put(block, top, bottom):
    return jnp.pad(block, ((top, bottom),) + ((0, 0),) * (block.ndim - 1))


def shards(image, text, image_ids, text_ids, log_scale, bias):
    i0, t0 = pl.pallas_call(
        pack,
        out_shape=(tiles(MSG), tiles(MSG)),
        in_specs=vmem(4),
        out_specs=tuple(vmem(2)),
    )(image, text, image_ids.reshape(1, ROWS), text_ids.reshape(1, ROWS))

    c0 = jnp.concatenate([i0, send(i0, SWAP)], axis=0)
    z1 = send(c0, along_z(1))
    a = send(t0, first(1))
    b = send(t0, first(-1))
    c = send(t0, first(2))
    y0 = jnp.concatenate([t0, a, b, c], axis=0)
    z2 = send(z1, along_z(1))
    s1 = send(z1, SWAP)
    yp = send(y0, second(1))
    ym = send(y0, second(-1))
    z3 = send(z2, along_z(1))
    s2 = send(z2, SWAP)
    y2a = send(yp[: 2 * MSG], second(1))
    y2b = send(ym[2 * MSG :], second(-1))
    z4 = send(z3[:MSG], along_z(1))
    s3 = send(z3, SWAP)
    s4 = send(z4, SWAP)

    early = shapes_of(PIECES, range(N_TEXT))
    place = lax.axis_index("blk") * 4 + lax.axis_index("group")
    *_, gc, g1, g2, g3, g4, h1, h2, h3, h4, k0, kp, km, k2a, k2b = pl.pallas_call(
        lambda *refs: visit(PIECES, range(N_TEXT), *refs),
        out_shape=(jax.ShapeDtypeStruct((8, 128), F32),) + early,
        in_specs=vmem(3 + N_IMAGE + N_TEXT),
        out_specs=tuple(vmem(1 + len(early))),
        scratch_shapes=[pltpu.VMEM((SIDE, D), BF16)] * 4
        + [pltpu.VMEM((SIDE, SIDE), BF16)] * 2
        + [pltpu.VMEM((8, SIDE), F32)] * 2,
        compiler_params=pltpu.CompilerParams(vmem_limit_bytes=40 * 2**20),
        cost_estimate=cost(3 * SIDE * SIDE * D, 8 * SIDE * D),
    )(
        log_scale.reshape(1, 1), bias.reshape(1, 1), place.reshape(1, 1),
        c0, z1, z2, z3, z4, s1, s2, s3, s4,
        y0, yp, ym, y2a, y2b,
    )

    q4 = send(h4, SWAP)
    g4 = g4 + q4
    w4 = send(g4, along_z(-1))
    k2a, k2b = behind(g4, k2a, k2b)
    r2a = send(k2a, second(-1))
    r2b = send(k2b, second(1))
    q3 = send(h3, SWAP)
    w3 = send(g3 + q3 + put(w4, 0, MSG - 1), along_z(-1))
    rp = send(kp + put(r2a, 0, 64), second(-1))
    rm = send(km + put(r2b, 64, 0), second(1))
    q2 = send(h2, SWAP)
    q1 = send(h1, SWAP)
    w2 = send(g2 + q2 + w3, along_z(-1))
    w1 = send(g1 + q1 + w2, along_z(-1))
    k0 = k0 + rp + rm
    ra = send(k0[32:64], first(-1))
    rb = send(k0[64:96], first(1))
    rc = send(k0[96:128], first(2))
    grad_text = k0[:32] + ra + rb + rc
    other = send(gc[MSG - 1 :] + w1[MSG - 1 :], SWAP)
    grad_image, sums = pl.pallas_call(
        unpack,
        out_shape=(rows_of(ROWS), jax.ShapeDtypeStruct((8, 128), F32)),
        in_specs=vmem(3),
        out_specs=tuple(vmem(2)),
        compiler_params=pltpu.CompilerParams(vmem_limit_bytes=2 * 2**20),
    )(gc, w1, other)
    for route in (first, second):
        sums = (sums + send(sums, route(2))) + (send(sums, route(1)) + send(sums, route(-1)))
    statistics = jnp.sum(sums[:6].reshape(3, 256), axis=1) * (2.0**-26)
    return grad_image, grad_text, statistics


def solution(mesh):
    rows, ids = P(AXES, None), P(AXES)
    return jax.shard_map(
        shards,
        mesh=mesh,
        in_specs=(rows, rows, ids, ids, P(), P()),
        out_specs=(rows, rows, P()),
        check_vma=False,
    )
```
